32 devices in a mesh: req: 16 (over z, x, core), tp: 2 (over y).
Axes of the slice: x: 2, y: 2, z: 4, core: 2. Of those that a mesh axis runs over, the one named last changes fastest.
Arguments:
- tokens: bfloat16 [32, 512, 2048], P('req'), may hold values from -6 to 6
- qkv_master: float32 [2048, 3, 2048], P('req', None, 'tp')
- q_gain: float32 [2048], P('tp')
- k_gain: float32 [2048], P('tp')
- lengths: int32 [32], P('req'), may hold values from 1 to 512, as said below
- page_holder: int32 [32, 4], P('req'), may hold values from 0 to 15, as said below
- page_slot: int32 [32, 4], P('req'), may hold values from 0 to 2, as said below
Outputs:
- attended: bfloat16 [32, 512, 2048], P('req', None, 'tp')
- kv_cache: bfloat16 [144, 2, 128, 2048], P('req', None, None, 'tp')
The draws below stay inside these ranges and needn't reach their ends.
Inputs may be any that keep to these rules, and one draw needn't show every extreme that they name: lengths[r] is at least 1; some prompt has exactly 512 tokens. page_holder[r, p] is r // 2, or the index just before or just after it along req, cyclically. The live pages of one req index's prompts that go to one holder have distinct page_slot values, so at most 3 of them; some req index sends 3 live pages to one holder.
All inputs are finite; a program needn't handle non-finite values.
Results may differ from the reference program's by a relative error of at most 0.009.
Values may be sent and summed in bfloat16 or wider, within the bound.
A program may use at most 128 MiB of HBM per device.

```python
import math
import jax
import jax.numpy as jnp
from jax import lax

D = 2048
HEADS = 16
HD = 128
LEN = 512
PAGE = 128
REQ_DEV = 2
QDIM = 2048
PAGES = 4
CAP = 3
SLOTS = 9
REQS = 32
N_REQ = 16


def table_draw(key):
    first_factor = jax.random.randint(jax.random.fold_in(key, 101), (REQS,), 1, LEN + 1)
    second_factor = jax.random.randint(jax.random.fold_in(key, 102), (REQS,), 1, LEN + 1)
    chosen = jax.random.randint(jax.random.fold_in(key, 103), (), 0, REQS)
    request_ids = jnp.arange(REQS, dtype=jnp.int32)
    drawn_lengths = LEN + 1 - jnp.maximum(first_factor * second_factor // LEN, 1)
    drawn_lengths = jnp.where(request_ids == chosen, LEN, drawn_lengths).astype(jnp.int32)
    per_device = REQ_DEV * PAGES
    priority = jax.random.randint(jax.random.fold_in(key, 104), (N_REQ, SLOTS), 0, 1 << 20) * SLOTS + jnp.arange(SLOTS, dtype=jnp.int32)[None, :]
    slot_order = jnp.argsort(priority, axis=1)[:, :per_device].astype(jnp.int32)
    local_index = jnp.arange(per_device, dtype=jnp.int32)
    forced = SLOTS - 1 - (local_index - chosen % REQ_DEV * PAGES + per_device) % per_device
    device_ids = jnp.arange(N_REQ, dtype=jnp.int32)[:, None]
    slot_ids = jnp.where(device_ids == chosen // REQ_DEV, forced[None, :], slot_order)
    offsets = slot_ids // CAP - 1
    holders = (device_ids + offsets + N_REQ) % N_REQ
    within = slot_ids % CAP
    return (drawn_lengths, holders.reshape(REQS, PAGES).astype(jnp.int32), within.reshape(REQS, PAGES).astype(jnp.int32))


def draw_lengths(key, part):
    return table_draw(key)[0]


def draw_page_holder(key, part):
    return table_draw(key)[1]


def draw_page_slot(key, part):
    return table_draw(key)[2]


def draw_qkv_master(key, part):
    scale = D ** (-0.5)
    return jax.random.normal(jax.random.fold_in(key, 201), (D, 3, QDIM), jnp.float32) * scale


def gain_draw(key, salt):
    return jnp.exp(jax.random.uniform(jax.random.fold_in(key, salt), (QDIM,), jnp.float32, math.log(0.5), math.log(2.0)))


def draw_q_gain(key, part):
    return gain_draw(key, 302)


def draw_k_gain(key, part):
    return gain_draw(key, 303)


def block_scale(key, extent, pieces, smallest, largest):
    loudness, own = 1.0, jax.random.fold_in(key, 6)
    for position, shards_of in pieces:
        draws = jnp.exp(jax.random.uniform(jax.random.fold_in(own, position), (shards_of,), jnp.float32, smallest / len(pieces), largest / len(pieces)))
        loudness = loudness * jnp.repeat(draws, extent[position] // shards_of).reshape([-1 if axis == position else 1 for axis in range(len(extent))])
    return loudness


def centred(own_key, dims, width, most, cuts=(), kind=jnp.bfloat16):
    loudness = block_scale(own_key, dims, cuts, -0.22, 0.18) if cuts else 1.0
    drawn = jax.random.normal(own_key, dims, jnp.float32) * width * loudness
    return jnp.minimum(jnp.maximum(drawn, -most), most).astype(kind)


def setup_inputs(seed: int = 0) -> dict:
    splits = jax.random.split(jax.random.key(seed), 8)
    return {
        "tokens": centred(splits[0], (REQS, LEN, D), 1.0, 6.0, ((0, 16),)),
        "qkv_master": draw_qkv_master(jax.random.fold_in(splits[7], 71), 0),
        "q_gain": draw_q_gain(jax.random.fold_in(splits[7], 71), 0),
        "k_gain": draw_k_gain(jax.random.fold_in(splits[7], 71), 0),
        "lengths": draw_lengths(jax.random.fold_in(splits[7], 71), 0),
        "page_holder": draw_page_holder(jax.random.fold_in(splits[7], 71), 0),
        "page_slot": draw_page_slot(jax.random.fold_in(splits[7], 71), 0),
    }


norm_epsilon = 1e-06
rope_theta = 500000.0

def rotate(values_in, seq_len, head_size):
    half_size = head_size // 2
    positions = jnp.arange(seq_len).astype(jnp.float32)
    frequency = rope_theta ** (-jnp.arange(half_size).astype(jnp.float32) * 2.0 / head_size)
    angles = positions[:, None] * frequency[None, :]
    cosine_table = jnp.cos(angles)[:, None, :]
    sine_table = jnp.sin(angles)[:, None, :]
    front_half = values_in[..., :half_size]
    back_half = values_in[..., half_size:]
    return jnp.concatenate([front_half * cosine_table - back_half * sine_table, back_half * cosine_table + front_half * sine_table], -1)

def attend(queries, key_rows, value_rows, length):
    seq_len = queries.shape[0]
    scores = jnp.einsum('thd,uhd->htu', queries.astype(jnp.float32), key_rows.astype(jnp.float32)) * HD ** (-0.5)
    query_pos = jnp.arange(seq_len).astype(jnp.int32)[:, None]
    key_pos = jnp.arange(seq_len).astype(jnp.int32)[None, :]
    allowed = (key_pos <= query_pos) & (key_pos < length)
    scores = jnp.where(allowed[None], scores, -1e+30)
    row_max = lax.optimization_barrier(jnp.max(scores, axis=-1, keepdims=True))
    exp_terms = jnp.where(allowed[None], jnp.exp(scores - row_max), 0.0)
    probs = (exp_terms / lax.optimization_barrier(jnp.sum(exp_terms, axis=-1, keepdims=True))).astype(jnp.bfloat16)
    output = jnp.einsum('htu,uhd->thd', probs.astype(jnp.float32), value_rows.astype(jnp.float32))
    keep_rows = jnp.arange(seq_len).astype(jnp.int32)[:, None, None] < length
    return jnp.where(keep_rows, output, 0.0).astype(jnp.bfloat16)

def reference(tokens, qkv_master, q_gain, k_gain, lengths, page_holder, page_slot):
    weight = qkv_master.astype(jnp.bfloat16).reshape(D, 3 * QDIM)

    def single_request(request_item):
        token_rows, length = request_item
        projected = jnp.dot(token_rows, weight, preferred_element_type=jnp.float32)
        queries = projected[:, :QDIM]
        key_rows = projected[:, QDIM:2 * QDIM]
        values = projected[:, 2 * QDIM:]
        queries = queries * lax.rsqrt(lax.optimization_barrier(jnp.mean(queries * queries, -1, keepdims=True)) + norm_epsilon) * q_gain
        key_rows = key_rows * lax.rsqrt(lax.optimization_barrier(jnp.mean(key_rows * key_rows, -1, keepdims=True)) + norm_epsilon) * k_gain
        q_rot = rotate(queries.reshape(LEN, HEADS, HD), LEN, HD).astype(jnp.bfloat16)
        k_rot = rotate(key_rows.reshape(LEN, HEADS, HD), LEN, HD).astype(jnp.bfloat16)
        v_round = values.astype(jnp.bfloat16).reshape(LEN, HEADS, HD)
        output = attend(q_rot, k_rot, v_round, length)
        return (output.reshape(LEN, QDIM), k_rot.reshape(LEN, QDIM), v_round.reshape(LEN, QDIM))
    attended, keys_all, values_all = lax.map(single_request, (tokens, lengths))
    page_blocks = jnp.stack([keys_all.reshape(REQS, PAGES, PAGE, QDIM), values_all.reshape(REQS, PAGES, PAGE, QDIM)], axis=2)
    is_live = (jnp.arange(PAGES).astype(jnp.int32) * PAGE)[None, :] < lengths[:, None]
    home_index = (jnp.arange(REQS).astype(jnp.int32) // REQ_DEV)[:, None]
    offset = (page_holder - home_index + 1 + N_REQ) % N_REQ - 1
    target = jnp.where(is_live, page_holder * SLOTS + (offset + 1) * CAP + page_slot, N_REQ * SLOTS)
    cache_rows = jnp.zeros((N_REQ * SLOTS + 1, 2, PAGE, QDIM), jnp.bfloat16)
    cache_rows = cache_rows.at[target.reshape(-1)].set(page_blocks.reshape(REQS * PAGES, 2, PAGE, QDIM))
    return (attended, cache_rows[:N_REQ * SLOTS])
```

```python
import functools

import jax
import jax.numpy as jnp
from jax import lax
from jax.experimental import pallas as pl
from jax.experimental.pallas import tpu as pltpu
from jax.sharding import PartitionSpec as P

HD = 128
PAGE = 128
CAP = 3
SLOTS = 9
STREAMS = 6
MESH = pl.DeviceIdType.MESH
VMEM_LIMIT = 56 * 1024 * 1024

norm_epsilon = 1e-06
rope_theta = 500000.0


def project_kernel(
    n, full_width, seq_len,
    tok, wown, cos_t, sin_t, q_gain, k_gain,
    q_out, k_out, v_out,
    weight, acc, ss_local, ss_remote,
    ring_send, ring_recv, sib_send, sib_recv, x_send, x_recv,
):
    rows = wown.shape[1]
    half = wown.shape[2]
    token_rows, width = tok.shape
    chips = n // 2
    column = chips // 2
    me, tp = lax.axis_index("req"), lax.axis_index("tp")
    chip, core = me // 2, me % 2
    side, level = chip % 2, chip // 2
    place = level * (1 - side) + (chips - 1 - level) * side

    def chip_at(position):
        p = (position + 2 * chips) % chips
        u = p // column
        return 2 * (p * (1 - u) + (chips - 1 - p) * u) + u

    following = (chip_at(place + 1) * 2 + core, tp)
    preceding = (chip_at(place - 1) * 2 + core, tp)
    sibling = (chip * 2 + 1 - core, tp)
    other = (me, 1 - tp)
    onward = (following, preceding)

    def owner(direction, step):
        return chip_at(place - step + 2 * direction * step)

    def chunk(u, chip_index, core_index):
        start = pl.multiple_of((chip_index * 2 + core_index) * rows, 16)
        return weight.at[u, pl.ds(start, rows), :]

    def ring(u, step):
        piece = chunk(u, owner(u % 2, step - 1), core)
        return pltpu.make_async_remote_copy(
            piece, piece, ring_send.at[u, step], ring_recv.at[u, step],
            device_id=onward[u % 2], device_id_type=MESH,
        )

    def ring_in(u, step):
        piece = chunk(u, owner(u % 2, step), core)
        return pltpu.make_async_remote_copy(
            piece, piece, ring_send.at[u, step], ring_recv.at[u, step],
            device_id=onward[u % 2], device_id_type=MESH,
        )

    def sib(u, step, whose):
        piece = chunk(u, owner(u % 2, step), whose)
        return pltpu.make_async_remote_copy(
            piece, piece, sib_send.at[u, step], sib_recv.at[u, step],
            device_id=sibling, device_id_type=MESH,
        )

    fused = (2 * rows) % 256 == 0
    tile = 256

    def multiply(step, first):
        for u in range(STREAMS):
            sib(u, step, 1 - core).wait_recv()
            if not fused:
                continue
            start = pl.multiple_of(owner(u % 2, step) * 2 * rows, 256)

            def one(i, carry, u=u, start=start):
                at = pl.multiple_of(i * tile, tile)
                part = jnp.dot(
                    tok[pl.ds(at, tile), pl.ds(start, 2 * rows)],
                    weight[u, pl.ds(start, 2 * rows), :],
                    preferred_element_type=jnp.float32,
                )
                if first:
                    acc[u, pl.ds(at, tile), :] = part
                else:
                    acc[u, pl.ds(at, tile), :] += part
                return carry

            lax.fori_loop(0, token_rows // tile, one, 0)

    own_start = pl.multiple_of(me * rows, 16)
    for u in range(STREAMS):
        weight[u, pl.ds(own_start, rows), :] = wown[u]

    barrier = pltpu.get_barrier_semaphore()
    for device in (following, preceding, sibling, other):
        pl.semaphore_signal(barrier, inc=1, device_id=device, device_id_type=MESH)
    pl.semaphore_wait(barrier, 4)

    for u in range(STREAMS):
        ring(u, 1).start()
    for u in range(STREAMS):
        sib(u, 0, core).start()
    multiply(0, True)

    def middle(step, carry):
        for u in range(STREAMS):
            ring_in(u, step).wait_recv()
            ring(u, step + 1).start()
            sib(u, step, core).start()
        multiply(step, False)
        return carry

    lax.fori_loop(1, chips - 1, middle, 0)
    last = chips - 1
    for u in range(STREAMS):
        ring_in(u, last).wait_recv()
        sib(u, last, core).start()
    multiply(last, False)

    if not fused:
        for u in range(STREAMS):

            def whole(i, carry, u=u):
                at = pl.multiple_of(i * tile, tile)
                acc[u, pl.ds(at, tile), :] = jnp.dot(
                    tok[pl.ds(at, tile), :], weight[u], preferred_element_type=jnp.float32
                )
                return carry

            lax.fori_loop(0, token_rows // tile, whole, 0)

    block = 128
    lanes = lax.broadcasted_iota(jnp.int32, (block, 128), 1)

    def squares(i, carry):
        at = pl.multiple_of(i * block, block)

        def total(first_stream):
            a = acc[first_stream, pl.ds(at, block), :]
            b = acc[first_stream + 1, pl.ds(at, block), :]
            return jnp.sum(a * a + b * b, axis=-1, keepdims=True)

        placed = jnp.where(lanes == 0, total(4), jnp.where(lanes == 1, total(0), 0.0))
        ss_local[:, pl.ds(at, block)] = placed.T[:8, :]
        return carry

    lax.fori_loop(0, token_rows // block, squares, 0)
    exchange = pltpu.make_async_remote_copy(
        ss_local, ss_remote, x_send, x_recv, device_id=other, device_id_type=MESH
    )
    exchange.start()

    def write_values(i, carry):
        at = pl.multiple_of(i * block, block)
        for part in range(2):
            v_out[pl.ds(at, block), part * half : (part + 1) * half] = acc[
                2 + part, pl.ds(at, block), :
            ].astype(jnp.bfloat16)
        return carry

    lax.fori_loop(0, token_rows // block, write_values, 0)
    exchange.wait()

    def turn(i, carry):
        at = pl.multiple_of(i * block, block)
        spot = pl.multiple_of((i * block) % seq_len, block)
        sums = ss_local[:, pl.ds(at, block)] + ss_remote[:, pl.ds(at, block)]
        scale = lax.rsqrt(sums / full_width + norm_epsilon)
        scale = jnp.concatenate([scale, jnp.zeros((block - 8, 128), jnp.float32)], 0).T
        cosine = cos_t[pl.ds(spot, block), :]
        sine = sin_t[pl.ds(spot, block), :]
        for base, lane, gain, out in ((4, 0, q_gain, q_out), (0, 1, k_gain, k_out)):
            factor = scale[:, lane : lane + 1]
            for part in range(2):
                for c in range(half // HD):
                    h = slice(part * half + c * HD, part * half + (c + 1) * HD)
                    x = acc[base + part, pl.ds(at, block), c * HD : (c + 1) * HD]
                    x = x * factor * gain[:, h]
                    y = x * cosine + pltpu.roll(x, HD // 2, 1) * sine
                    out[pl.ds(at, block), h] = y.astype(jnp.bfloat16)
        return carry

    lax.fori_loop(0, token_rows // block, turn, 0)

    def drain(step, carry):
        for u in range(STREAMS):
            ring(u, step).wait_send()
        return carry

    lax.fori_loop(1, chips, drain, 0)

    def drain_sib(step, carry):
        for u in range(STREAMS):
            sib(u, step, core).wait_send()
        return carry

    lax.fori_loop(0, chips, drain_sib, 0)


def attention_kernel(lengths, q, k, v, out):
    length = lengths[pl.program_id(0)]
    seq_len = q.shape[0]
    step = 128
    for h in range(q.shape[1] // HD):
        hs = slice(h * HD, (h + 1) * HD)
        for b in range(seq_len // step):
            rows, count = slice(b * step, (b + 1) * step), (b + 1) * step
            scores = lax.dot_general(
                q[rows, hs], k[:count, hs], (((1,), (1,)), ((), ())),
                preferred_element_type=jnp.float32,
            ) * HD ** (-0.5)
            query_pos = lax.broadcasted_iota(jnp.int32, (step, count), 0) + b * step
            key_pos = lax.broadcasted_iota(jnp.int32, (step, count), 1)
            allowed = (key_pos <= query_pos) & (key_pos < length)
            scores = jnp.where(allowed, scores, -1e30)
            top = jnp.max(scores, axis=-1, keepdims=True)
            terms = jnp.exp(scores - top)
            total = jnp.sum(terms, axis=-1, keepdims=True)
            mixed = jnp.dot(
                terms.astype(jnp.bfloat16), v[:count, hs], preferred_element_type=jnp.float32
            ) / total
            row = lax.broadcasted_iota(jnp.int32, (step, HD), 0) + b * step
            out[rows, hs] = jnp.where(row < length, mixed, 0.0).astype(jnp.bfloat16)


def pack_kernel(index, valid, k, v, out):
    keep = valid[pl.program_id(0)] > 0
    zero = jnp.zeros(k.shape, k.dtype)
    out[0, 0] = jnp.where(keep, k[...], zero)
    out[0, 1] = jnp.where(keep, v[...], zero)


def pack(k, v, index, valid):
    width = k.shape[1]
    return pl.pallas_call(
        pack_kernel,
        grid_spec=pltpu.PrefetchScalarGridSpec(
            num_scalar_prefetch=2,
            grid=(CAP,),
            in_specs=[pl.BlockSpec((PAGE, width), lambda s, index, valid: (index[s], 0))] * 2,
            out_specs=pl.BlockSpec((1, 2, PAGE, width), lambda s, index, valid: (s, 0, 0, 0)),
        ),
        out_shape=jax.ShapeDtypeStruct((CAP, 2, PAGE, width), k.dtype),
    )(index, valid, k, v)


def assemble_kernel(index, valid, k, v, low, high, out):
    s = pl.program_id(0)
    keep = valid[s] > 0

    @pl.when(s < CAP)
    def _():
        out[...] = high[...]

    @pl.when((s >= CAP) & (s < 2 * CAP))
    def _():
        zero = jnp.zeros(k.shape, k.dtype)
        out[0, 0] = jnp.where(keep, k[...], zero)
        out[0, 1] = jnp.where(keep, v[...], zero)

    @pl.when(s >= 2 * CAP)
    def _():
        out[...] = low[...]


def assemble(k, v, low, high, index, valid):
    width = k.shape[1]
    own = jnp.concatenate([jnp.full((CAP,), index[CAP]), index[CAP : 2 * CAP], jnp.full((CAP,), index[2 * CAP - 1])])
    block = (1, 2, PAGE, width)
    page = pl.BlockSpec((PAGE, width), lambda s, index, valid: (index[s], 0))
    return pl.pallas_call(
        assemble_kernel,
        grid_spec=pltpu.PrefetchScalarGridSpec(
            num_scalar_prefetch=2,
            grid=(SLOTS,),
            in_specs=[
                page,
                page,
                pl.BlockSpec(block, lambda s, index, valid: (jnp.maximum(s - 2 * CAP, 0), 0, 0, 0)),
                pl.BlockSpec(block, lambda s, index, valid: (jnp.minimum(s, CAP - 1), 0, 0, 0)),
            ],
            out_specs=pl.BlockSpec(block, lambda s, index, valid: (s, 0, 0, 0)),
        ),
        out_shape=jax.ShapeDtypeStruct((SLOTS, 2, PAGE, width), k.dtype),
    )(own, valid, k, v, low, high)


def body(tokens, qkv_master, q_gain, k_gain, lengths, page_holder, page_slot):
    req_dev, seq_len, model_width = tokens.shape
    row_share, _, q_local = qkv_master.shape
    half = q_local // 2
    count = lax.axis_size("req")
    chips = count // 2
    token_rows = tokens.reshape(req_dev * seq_len, model_width)
    own = jnp.concatenate([qkv_master[:, 1:], qkv_master[:, :1]], 1).astype(jnp.bfloat16)
    own = own.reshape(row_share, STREAMS, half).transpose(1, 0, 2)

    frequency = rope_theta ** (-jnp.arange(HD // 2).astype(jnp.float32) * 2.0 / HD)
    angles = jnp.arange(seq_len).astype(jnp.float32)[:, None] * frequency[None, :]
    cosine, sine = jnp.cos(angles), jnp.sin(angles)
    cosine = jnp.concatenate([cosine, cosine], -1)
    sine = jnp.concatenate([-sine, sine], -1)

    vmem = pl.BlockSpec(memory_space=pltpu.VMEM)
    flat = jax.ShapeDtypeStruct((req_dev * seq_len, q_local), jnp.bfloat16)
    q, k, v = pl.pallas_call(
        functools.partial(project_kernel, count, q_local * lax.axis_size("tp"), seq_len),
        out_shape=(flat, flat, flat),
        in_specs=[vmem] * 6,
        out_specs=(vmem, vmem, vmem),
        scratch_shapes=[
            pltpu.VMEM((STREAMS, model_width, half), jnp.bfloat16),
            pltpu.VMEM((STREAMS, req_dev * seq_len, half), jnp.float32),
            pltpu.VMEM((8, req_dev * seq_len), jnp.float32),
            pltpu.VMEM((8, req_dev * seq_len), jnp.float32),
            pltpu.SemaphoreType.DMA((STREAMS, chips)),
            pltpu.SemaphoreType.DMA((STREAMS, chips)),
            pltpu.SemaphoreType.DMA((STREAMS, chips)),
            pltpu.SemaphoreType.DMA((STREAMS, chips)),
            pltpu.SemaphoreType.DMA,
            pltpu.SemaphoreType.DMA,
        ],
        compiler_params=pltpu.CompilerParams(
            collective_id=0, has_side_effects=True, vmem_limit_bytes=VMEM_LIMIT
        ),
    )(token_rows, own, cosine, sine, q_gain[None, :], k_gain[None, :])

    page_count = seq_len // PAGE
    home = lax.axis_index("req")
    live = (jnp.arange(page_count) * PAGE)[None, :] < lengths[:, None]
    offset = (page_holder - home + 1 + count) % count - 1
    target = jnp.where(live, (offset + 1) * CAP + page_slot, -1).reshape(-1)
    match = target[None, :] == jnp.arange(SLOTS)[:, None]
    valid = jnp.any(match, 1).astype(jnp.int32)
    index = jnp.sum(match * jnp.arange(req_dev * page_count)[None, :], 1).astype(jnp.int32)

    forward = [(i, (i + 1) % count) for i in range(count)]
    backward = [(j, i) for i, j in forward]
    low = lax.ppermute(pack(k, v, index[2 * CAP :], valid[2 * CAP :]), "req", forward)
    high = lax.ppermute(pack(k, v, index[:CAP], valid[:CAP]), "req", backward)

    heads = q_local // HD
    group = 4
    spec = pl.BlockSpec((seq_len, group * HD), lambda r, h, lengths: (r, h))
    attended = pl.pallas_call(
        attention_kernel,
        grid_spec=pltpu.PrefetchScalarGridSpec(
            num_scalar_prefetch=1,
            grid=(req_dev, heads // group),
            in_specs=[spec] * 3,
            out_specs=spec,
        ),
        out_shape=flat,
        cost_estimate=pl.CostEstimate(
            flops=8 * req_dev * heads * seq_len * seq_len * HD,
            bytes_accessed=8 * req_dev * seq_len * q_local,
            transcendentals=req_dev * heads * seq_len * seq_len,
        ),
    )(lengths, q, k, v)

    kv_cache = assemble(k, v, low, high, index, valid)
    return attended.reshape(req_dev, seq_len, q_local), kv_cache


def solution(mesh):
    in_specs = (
        P("req", None, None),
        P("req", None, "tp"),
        P("tp"),
        P("tp"),
        P("req"),
        P("req", None),
        P("req", None),
    )
    out_specs = (P("req", None, "tp"), P("req", None, None, "tp"))
    return jax.shard_map(body, mesh=mesh, in_specs=in_specs, out_specs=out_specs, check_vma=False)
```

```python
import functools

import jax
import jax.numpy as jnp
import numpy as np
from jax import lax
from jax.experimental import pallas as pl
from jax.experimental.pallas import tpu as pltpu
from jax.sharding import PartitionSpec as P

HD = 128
PAGE = 128
CAP = 3
SLOTS = 9
STREAMS = 6
LAG = 2
MESH = pl.DeviceIdType.MESH
VMEM_LIMIT = 56 * 1024 * 1024

norm_epsilon = 1e-06
rope_theta = 500000.0


def prefill_kernel(
    n, full_width, seq_len,
    lengths, chosen, tok, master, cos_t, sin_t, q_gain, k_gain,
    attended, cache,
    weight, acc, q_rows, k_rows, v_rows, pages, ss_local, ss_remote,
    ring_send, ring_recv, sib_send, sib_recv, x_send, x_recv, page_send, page_recv, own_sem,
):
    rows = master.shape[1]
    half = weight.shape[2]
    token_rows, width = tok.shape
    chips = n // 2
    column = chips // 2
    me, tp = lax.axis_index("req"), lax.axis_index("tp")
    chip, core = me // 2, me % 2
    side, level = chip % 2, chip // 2
    place = level * (1 - side) + (chips - 1 - level) * side

    def chip_at(position):
        p = (position + 2 * chips) % chips
        u = p // column
        return 2 * (p * (1 - u) + (chips - 1 - p) * u) + u

    following = (chip_at(place + 1) * 2 + core, tp)
    preceding = (chip_at(place - 1) * 2 + core, tp)
    sibling = (chip * 2 + 1 - core, tp)
    other = (me, 1 - tp)
    onward = (following, preceding)
    before = ((me + n - 1) % n, tp)
    after = ((me + 1) % n, tp)

    def owner(direction, step):
        return chip_at(place - step + 2 * direction * step)

    def chunk(u, chip_index, core_index):
        start = pl.multiple_of((chip_index * 2 + core_index) * rows, 16)
        return weight.at[u, pl.ds(start, rows), :]

    def ring(u, step):
        piece = chunk(u, owner(u % 2, step - 1), core)
        return pltpu.make_async_remote_copy(
            piece, piece, ring_send.at[u, step], ring_recv.at[u, step],
            device_id=onward[u % 2], device_id_type=MESH,
        )

    def ring_in(u, step):
        piece = chunk(u, owner(u % 2, step), core)
        return pltpu.make_async_remote_copy(
            piece, piece, ring_send.at[u, step], ring_recv.at[u, step],
            device_id=onward[u % 2], device_id_type=MESH,
        )

    def sib(u, step, whose):
        piece = chunk(u, owner(u % 2, step), whose)
        return pltpu.make_async_remote_copy(
            piece, piece, sib_send.at[u, step], sib_recv.at[u, step],
            device_id=sibling, device_id_type=MESH,
        )

    fused = (2 * rows) % 256 == 0
    tile = 256

    def multiply(u, step):
        sib(u, step, 1 - core).wait_recv()
        if not fused:
            return
        start = pl.multiple_of(owner(u % 2, step) * 2 * rows, 256)

        def one(i, carry):
            at = pl.multiple_of(i * tile, tile)
            acc[u, pl.ds(at, tile), :] += jnp.dot(
                tok[pl.ds(at, tile), pl.ds(start, 2 * rows)],
                weight[u, pl.ds(start, 2 * rows), :],
                preferred_element_type=jnp.float32,
            )
            return carry

        lax.fori_loop(0, token_rows // tile, one, 0)

    own_start = pl.multiple_of(me * rows, 16)
    for u in range(STREAMS):
        at = (u % 2) * half
        weight[u, pl.ds(own_start, rows), :] = master[2 - u // 2, :, at : at + half].astype(jnp.bfloat16)

    barrier = pltpu.get_barrier_semaphore()
    for device in (following, preceding, sibling, other, before, after):
        pl.semaphore_signal(barrier, inc=1, device_id=device, device_id_type=MESH)
    pl.semaphore_wait(barrier, 6)

    for u in range(STREAMS):
        ring(u, 1).start()
    for u in range(STREAMS):
        sib(u, 0, core).start()

    def clear(i, carry):
        at = pl.multiple_of(i * 64, 64)
        for u in range(STREAMS):
            acc[u, pl.ds(at, 64), :] = jnp.zeros((64, half), jnp.float32)
        return carry

    lax.fori_loop(0, token_rows // 64, clear, 0)
    for u in range(STREAMS - LAG):
        multiply(u, 0)

    def middle(step, carry):
        for u in range(STREAMS):
            ring_in(u, step).wait_recv()
            ring(u, step + 1).start()
            sib(u, step, core).start()
            if u < LAG:
                multiply(u - LAG + STREAMS, step - 1)
            else:
                multiply(u - LAG, step)
        return carry

    lax.fori_loop(1, chips - 1, middle, 0)

    def whole(u):
        def one(i, carry):
            at = pl.multiple_of(i * tile, tile)
            acc[u, pl.ds(at, tile), :] = jnp.dot(
                tok[pl.ds(at, tile), :], weight[u], preferred_element_type=jnp.float32
            )
            return carry

        if not fused:
            lax.fori_loop(0, token_rows // tile, one, 0)

    block = 128

    def send_page(kind, direction, slot):
        return pltpu.make_async_remote_copy(
            pages.at[kind, 2 * direction, slot],
            cache.at[2 * direction * CAP + slot, kind],
            page_send.at[kind, direction, slot],
            page_recv.at[kind, direction, slot],
            device_id=(before, after)[direction], device_id_type=MESH,
        )

    def keep_page(kind, slot):
        return pltpu.make_async_copy(
            pages.at[kind, 1, slot], cache.at[CAP + slot, kind], own_sem.at[kind, slot]
        )

    candidates = token_rows // PAGE

    def publish(kind, source):
        for which in (0, 2, 1):

            def fill(i, carry, which=which):
                at = pl.multiple_of(i * 16, 16)
                sums = [None] * CAP
                for p in range(candidates):
                    rows_p = pl.ds(pl.multiple_of(p * PAGE + at, 16), 16)
                    page = source[rows_p, :]
                    for slot in range(CAP):
                        share = chosen[(which * CAP + slot) * candidates + p]
                        term = page * jnp.full(page.shape, share, jnp.float32).astype(page.dtype)
                        sums[slot] = term if p == 0 else sums[slot] + term
                for slot in range(CAP):
                    pages[kind, which, slot, pl.ds(at, 16), :] = sums[slot]
                return carry

            lax.fori_loop(0, PAGE // 16, fill, 0)
            for slot in range(CAP):
                if which == 1:
                    keep_page(kind, slot).start()
                else:
                    send_page(kind, which // 2, slot).start()

    def write_values(i, carry):
        at = pl.multiple_of(i * block, block)
        for part in range(2):
            v_rows[pl.ds(at, block), part * half : (part + 1) * half] = acc[
                part, pl.ds(at, block), :
            ].astype(jnp.bfloat16)
        return carry

    def values_ready():
        whole(0)
        whole(1)
        lax.fori_loop(0, token_rows // block, write_values, 0)
        publish(1, v_rows)

    last = chips - 1
    for u in range(STREAMS):
        ring_in(u, last).wait_recv()
        sib(u, last, core).start()
        if u < LAG:
            multiply(u - LAG + STREAMS, last - 1)
        else:
            multiply(u - LAG, last)
        if u - LAG == 1:
            values_ready()
    for u in range(STREAMS - LAG, STREAMS):
        multiply(u, last)
    for u in range(2, STREAMS):
        whole(u)

    lanes = lax.broadcasted_iota(jnp.int32, (block, 128), 1)

    def squares(i, carry):
        at = pl.multiple_of(i * block, block)

        def total(first_stream):
            a = acc[first_stream, pl.ds(at, block), :]
            b = acc[first_stream + 1, pl.ds(at, block), :]
            return jnp.sum(a * a + b * b, axis=-1, keepdims=True)

        placed = jnp.where(lanes == 0, total(4), jnp.where(lanes == 1, total(2), 0.0))
        ss_local[:, pl.ds(at, block)] = placed.T[:8, :]
        return carry

    lax.fori_loop(0, token_rows // block, squares, 0)
    exchange = pltpu.make_async_remote_copy(
        ss_local, ss_remote, x_send, x_recv, device_id=other, device_id_type=MESH
    )
    exchange.start()
    exchange.wait()

    def turn(base, lane, gain, out):
        def one(i, carry):
            at = pl.multiple_of(i * block, block)
            spot = pl.multiple_of((i * block) % seq_len, block)
            sums = ss_local[:, pl.ds(at, block)] + ss_remote[:, pl.ds(at, block)]
            scale = lax.rsqrt(sums / full_width + norm_epsilon)
            scale = jnp.concatenate([scale, jnp.zeros((block - 8, 128), jnp.float32)], 0).T
            cosine = cos_t[pl.ds(spot, block), :]
            sine = sin_t[pl.ds(spot, block), :]
            factor = scale[:, lane : lane + 1]
            for part in range(2):
                for c in range(half // HD):
                    h = slice(part * half + c * HD, part * half + (c + 1) * HD)
                    x = acc[base + part, pl.ds(at, block), c * HD : (c + 1) * HD]
                    x = x * factor * gain[:, h]
                    y = x * cosine + pltpu.roll(x, HD // 2, 1) * sine
                    out[pl.ds(at, block), h] = y.astype(jnp.bfloat16)
            return carry

        lax.fori_loop(0, token_rows // block, one, 0)

    turn(2, 1, k_gain, k_rows)
    publish(0, k_rows)
    turn(4, 0, q_gain, q_rows)

    heads = 2 * half // HD
    step_rows = 128

    def attend(i, carry):
        r, h = i // heads, i % heads
        length = lengths[r]
        top_row = pl.multiple_of(r * seq_len, seq_len)
        hs = pl.ds(pl.multiple_of(h * HD, HD), HD)
        for b in range(seq_len // step_rows):
            count = (b + 1) * step_rows
            rows_b = pl.ds(pl.multiple_of(top_row + b * step_rows, step_rows), step_rows)
            keys = pl.ds(top_row, count)
            scores = lax.dot_general(
                q_rows[rows_b, hs], k_rows[keys, hs], (((1,), (1,)), ((), ())),
                preferred_element_type=jnp.float32,
            ) * HD ** (-0.5)
            query_pos = lax.broadcasted_iota(jnp.int32, (step_rows, count), 0) + b * step_rows
            key_pos = lax.broadcasted_iota(jnp.int32, (step_rows, count), 1)
            allowed = (key_pos <= query_pos) & (key_pos < length)
            scores = jnp.where(allowed, scores, -1e30)
            terms = jnp.exp(scores - jnp.max(scores, axis=-1, keepdims=True))
            mixed = jnp.dot(
                terms.astype(jnp.bfloat16), v_rows[keys, hs], preferred_element_type=jnp.float32
            ) / jnp.sum(terms, axis=-1, keepdims=True)
            row = lax.broadcasted_iota(jnp.int32, (step_rows, HD), 0) + b * step_rows
            attended[rows_b, hs] = jnp.where(row < length, mixed, 0.0).astype(jnp.bfloat16)
        return carry

    lax.fori_loop(0, token_rows // seq_len * heads, attend, 0)

    def drain(step, carry):
        for u in range(STREAMS):
            ring(u, step).wait_send()
        return carry

    lax.fori_loop(1, chips, drain, 0)

    def drain_sib(step, carry):
        for u in range(STREAMS):
            sib(u, step, core).wait_send()
        return carry

    lax.fori_loop(0, chips, drain_sib, 0)
    for kind in (1, 0):
        for slot in range(CAP):
            for direction in range(2):
                send_page(kind, direction, slot).wait()
            keep_page(kind, slot).wait()


def body(tokens, qkv_master, q_gain, k_gain, lengths, page_holder, page_slot):
    req_dev, seq_len, model_width = tokens.shape
    row_share, _, q_local = qkv_master.shape
    half = q_local // 2
    count = lax.axis_size("req")
    chips = count // 2
    rows = req_dev * seq_len
    token_rows = tokens.reshape(rows, model_width)

    frequency = np.float32(rope_theta) ** (-np.arange(HD // 2, dtype=np.float32) * np.float32(2.0 / HD))
    angles = np.arange(seq_len, dtype=np.float32)[:, None] * frequency[None, :]
    cosine, sine = np.cos(angles), np.sin(angles)
    cosine = jnp.asarray(np.concatenate([cosine, cosine], -1), jnp.float32)
    sine = jnp.asarray(np.concatenate([-sine, sine], -1), jnp.float32)

    page_count = seq_len // PAGE
    home = lax.axis_index("req")
    live = (jnp.arange(page_count) * PAGE)[None, :] < lengths[:, None]
    offset = (page_holder - home + 1 + count) % count - 1
    target = jnp.where(live, (offset + 1) * CAP + page_slot, -1).reshape(-1)
    match = target[None, :] == jnp.arange(SLOTS)[:, None]
    chosen = match.astype(jnp.float32).reshape(-1)

    vmem = pl.BlockSpec(memory_space=pltpu.VMEM)
    smem = pl.BlockSpec(memory_space=pltpu.SMEM)
    dma = pltpu.SemaphoreType.DMA
    attended, cache = pl.pallas_call(
        functools.partial(prefill_kernel, count, q_local * lax.axis_size("tp"), seq_len),
        out_shape=(
            jax.ShapeDtypeStruct((rows, q_local), jnp.bfloat16),
            jax.ShapeDtypeStruct((SLOTS, 2, PAGE, q_local), jnp.bfloat16),
        ),
        in_specs=[smem] * 2 + [vmem] * 6,
        out_specs=(vmem, pl.BlockSpec(memory_space=pl.ANY)),
        scratch_shapes=[
            pltpu.VMEM((STREAMS, model_width, half), jnp.bfloat16),
            pltpu.VMEM((STREAMS, rows, half), jnp.float32),
            pltpu.VMEM((rows, q_local), jnp.bfloat16),
            pltpu.VMEM((rows, q_local), jnp.bfloat16),
            pltpu.VMEM((rows, q_local), jnp.bfloat16),
            pltpu.VMEM((2, 3, CAP, PAGE, q_local), jnp.bfloat16),
            pltpu.VMEM((8, rows), jnp.float32),
            pltpu.VMEM((8, rows), jnp.float32),
            dma((STREAMS, chips)), dma((STREAMS, chips)),
            dma((STREAMS, chips)), dma((STREAMS, chips)),
            dma, dma,
            dma((2, 2, CAP)), dma((2, 2, CAP)), dma((2, CAP)),
        ],
        compiler_params=pltpu.CompilerParams(
            collective_id=0, has_side_effects=True, vmem_limit_bytes=VMEM_LIMIT
        ),
    )(lengths, chosen, token_rows, qkv_master.transpose(1, 0, 2), cosine, sine, q_gain[None, :], k_gain[None, :])
    return attended.reshape(req_dev, seq_len, q_local), cache


def solution(mesh):
    in_specs = (
        P("req", None, None),
        P("req", None, "tp"),
        P("tp"),
        P("tp"),
        P("req"),
        P("req", None),
        P("req", None),
    )
    out_specs = (P("req", None, "tp"), P("req", None, None, "tp"))
    return jax.shard_map(body, mesh=mesh, in_specs=in_specs, out_specs=out_specs, check_vma=False)
```

```python
import functools
import math

import jax
import jax.numpy as jnp
import numpy as np
from jax import lax
from jax.experimental import pallas as pl
from jax.experimental.pallas import tpu as pltpu
from jax.sharding import PartitionSpec as P

HD = 128
PAGE = 128
CAP = 3
SLOTS = 9
STREAMS = 6
LAG = 2
MESH = pl.DeviceIdType.MESH
VMEM_LIMIT = 56 * 1024 * 1024

norm_epsilon = 1e-06
rope_theta = 500000.0


def prefill_kernel(
    n, full_width, seq_len,
    lengths, chosen, tok, master, cos_t, sin_t, q_gain, k_gain,
    attended, cache,
    weight, acc, q_rows, k_rows, v_rows, pages, ss_local, ss_remote,
    ring_send, ring_recv, sib_send, sib_recv, x_send, x_recv, page_send, page_recv, own_sem,
):
    rows = master.shape[1]
    half = weight.shape[2]
    token_rows, width = tok.shape
    chips = n // 2
    column = chips // 2
    me, tp = lax.axis_index("req"), lax.axis_index("tp")
    chip, core = me // 2, me % 2
    side, level = chip % 2, chip // 2
    place = level * (1 - side) + (chips - 1 - level) * side

    def chip_at(position):
        p = (position + 2 * chips) % chips
        u = p // column
        return 2 * (p * (1 - u) + (chips - 1 - p) * u) + u

    following = (chip_at(place + 1) * 2 + core, tp)
    preceding = (chip_at(place - 1) * 2 + core, tp)
    sibling = (chip * 2 + 1 - core, tp)
    other = (me, 1 - tp)
    onward = (following, preceding)
    before = ((me + n - 1) % n, tp)
    after = ((me + 1) % n, tp)

    def owner(direction, step):
        return chip_at(place - step + 2 * direction * step)

    def chunk(u, chip_index, core_index):
        start = pl.multiple_of((chip_index * 2 + core_index) * rows, 16)
        return weight.at[u, pl.ds(start, rows), :]

    def ring(u, step):
        piece = chunk(u, owner(u % 2, step - 1), core)
        return pltpu.make_async_remote_copy(
            piece, piece, ring_send.at[u, step], ring_recv.at[u, step],
            device_id=onward[u % 2], device_id_type=MESH,
        )

    def ring_in(u, step):
        piece = chunk(u, owner(u % 2, step), core)
        return pltpu.make_async_remote_copy(
            piece, piece, ring_send.at[u, step], ring_recv.at[u, step],
            device_id=onward[u % 2], device_id_type=MESH,
        )

    def sib(u, step, whose):
        piece = chunk(u, owner(u % 2, step), whose)
        return pltpu.make_async_remote_copy(
            piece, piece, sib_send.at[u, step], sib_recv.at[u, step],
            device_id=sibling, device_id_type=MESH,
        )

    fused = (2 * rows) % 256 == 0
    tile = 256

    def multiply(u, step):
        sib(u, step, 1 - core).wait_recv()
        if not fused:
            return
        start = pl.multiple_of(owner(u % 2, step) * 2 * rows, 256)

        def one(i, carry):
            at = pl.multiple_of(i * tile, tile)
            acc[u, pl.ds(at, tile), :] += jnp.dot(
                tok[pl.ds(at, tile), pl.ds(start, 2 * rows)],
                weight[u, pl.ds(start, 2 * rows), :],
                preferred_element_type=jnp.float32,
            )
            return carry

        lax.fori_loop(0, token_rows // tile, one, 0)

    own_start = pl.multiple_of(me * rows, 16)
    for u in range(STREAMS):
        at = (u % 2) * half
        weight[u, pl.ds(own_start, rows), :] = master[2 - u // 2, :, at : at + half].astype(jnp.bfloat16)

    barrier = pltpu.get_barrier_semaphore()
    for device in (following, preceding, sibling, other, before, after):
        pl.semaphore_signal(barrier, inc=1, device_id=device, device_id_type=MESH)
    pl.semaphore_wait(barrier, 6)

    for u in range(STREAMS):
        ring(u, 1).start()
    for u in range(STREAMS):
        sib(u, 0, core).start()

    def clear(i, carry):
        at = pl.multiple_of(i * 64, 64)
        for u in range(STREAMS):
            acc[u, pl.ds(at, 64), :] = jnp.zeros((64, half), jnp.float32)
        return carry

    lax.fori_loop(0, token_rows // 64, clear, 0)
    for u in range(STREAMS - LAG):
        multiply(u, 0)

    def middle(step, carry):
        for u in range(STREAMS):
            ring_in(u, step).wait_recv()
            ring(u, step + 1).start()
            sib(u, step, core).start()
            if u < LAG:
                multiply(u - LAG + STREAMS, step - 1)
            else:
                multiply(u - LAG, step)
        return carry

    lax.fori_loop(1, chips - 1, middle, 0)

    def whole(u):
        def one(i, carry):
            at = pl.multiple_of(i * tile, tile)
            acc[u, pl.ds(at, tile), :] = jnp.dot(
                tok[pl.ds(at, tile), :], weight[u], preferred_element_type=jnp.float32
            )
            return carry

        if not fused:
            lax.fori_loop(0, token_rows // tile, one, 0)

    block = 128

    def send_page(kind, direction, slot):
        return pltpu.make_async_remote_copy(
            pages.at[kind, 2 * direction, slot],
            cache.at[2 * direction * CAP + slot, kind],
            page_send.at[kind, direction, slot],
            page_recv.at[kind, direction, slot],
            device_id=(before, after)[direction], device_id_type=MESH,
        )

    def keep_page(kind, slot):
        return pltpu.make_async_copy(
            pages.at[kind, 1, slot], cache.at[CAP + slot, kind], own_sem.at[kind, slot]
        )

    candidates = token_rows // PAGE

    def publish(kind, source):
        for which in (0, 2, 1):

            def fill(i, carry, which=which):
                at = pl.multiple_of(i * 16, 16)
                sums = [None] * CAP
                for p in range(candidates):
                    rows_p = pl.ds(pl.multiple_of(p * PAGE + at, 16), 16)
                    page = source[rows_p, :]
                    for slot in range(CAP):
                        share = chosen[(which * CAP + slot) * candidates + p]
                        term = page * jnp.full(page.shape, share, jnp.float32).astype(page.dtype)
                        sums[slot] = term if p == 0 else sums[slot] + term
                for slot in range(CAP):
                    pages[kind, which, slot, pl.ds(at, 16), :] = sums[slot]
                return carry

            lax.fori_loop(0, PAGE // 16, fill, 0)
            for slot in range(CAP):
                if which == 1:
                    keep_page(kind, slot).start()
                else:
                    send_page(kind, which // 2, slot).start()

    def write_values(i, carry):
        at = pl.multiple_of(i * block, block)
        for part in range(2):
            v_rows[pl.ds(at, block), part * half : (part + 1) * half] = acc[
                part, pl.ds(at, block), :
            ].astype(jnp.bfloat16)
        return carry

    def values_ready():
        whole(0)
        whole(1)
        lax.fori_loop(0, token_rows // block, write_values, 0)
        publish(1, v_rows)

    last = chips - 1
    for u in range(STREAMS):
        ring_in(u, last).wait_recv()
        sib(u, last, core).start()
        if u < LAG:
            multiply(u - LAG + STREAMS, last - 1)
        else:
            multiply(u - LAG, last)
        if u - LAG == 1:
            values_ready()
    for u in range(STREAMS - LAG, STREAMS):
        multiply(u, last)
    for u in range(2, STREAMS):
        whole(u)

    lanes = lax.broadcasted_iota(jnp.int32, (block, 128), 1)

    def squares(i, carry):
        at = pl.multiple_of(i * block, block)

        def total(first_stream):
            a = acc[first_stream, pl.ds(at, block), :]
            b = acc[first_stream + 1, pl.ds(at, block), :]
            return jnp.sum(a * a + b * b, axis=-1, keepdims=True)

        placed = jnp.where(lanes == 0, total(4), jnp.where(lanes == 1, total(2), 0.0))
        ss_local[:, pl.ds(at, block)] = placed.T[:8, :]
        return carry

    lax.fori_loop(0, token_rows // block, squares, 0)
    exchange = pltpu.make_async_remote_copy(
        ss_local, ss_remote, x_send, x_recv, device_id=other, device_id_type=MESH
    )
    exchange.start()
    exchange.wait()

    def turn(base, lane, gain, out):
        def one(i, carry):
            at = pl.multiple_of(i * block, block)
            spot = pl.multiple_of((i * block) % seq_len, block)
            sums = ss_local[:, pl.ds(at, block)] + ss_remote[:, pl.ds(at, block)]
            scale = lax.rsqrt(sums / full_width + norm_epsilon)
            scale = jnp.concatenate([scale, jnp.zeros((block - 8, 128), jnp.float32)], 0).T
            cosine = cos_t[pl.ds(spot, block), :]
            sine = sin_t[pl.ds(spot, block), :]
            factor = scale[:, lane : lane + 1]
            for part in range(2):
                for c in range(half // HD):
                    h = slice(part * half + c * HD, part * half + (c + 1) * HD)
                    x = acc[base + part, pl.ds(at, block), c * HD : (c + 1) * HD]
                    x = x * factor * gain[:, h]
                    y = x * cosine + pltpu.roll(x, HD // 2, 1) * sine
                    out[pl.ds(at, block), h] = y.astype(jnp.bfloat16)
            return carry

        lax.fori_loop(0, token_rows // block, one, 0)

    turn(2, 1, k_gain, k_rows)
    publish(0, k_rows)
    turn(4, 0, q_gain, q_rows)

    heads = 2 * half // HD
    step_rows = 128

    exponent = HD ** (-0.5) * math.log2(math.e)
    below = lax.broadcasted_iota(jnp.int32, (step_rows, step_rows), 1) <= lax.broadcasted_iota(
        jnp.int32, (step_rows, step_rows), 0
    )

    def attend(i, carry):
        r, h = i // heads, i % heads
        length = lengths[r]
        top_row = pl.multiple_of(r * seq_len, seq_len)
        hs = pl.ds(pl.multiple_of(h * HD, HD), HD)
        for b in range(seq_len // step_rows):
            count = (b + 1) * step_rows
            rows_b = pl.ds(pl.multiple_of(top_row + b * step_rows, step_rows), step_rows)
            keys = pl.ds(top_row, count)
            scores = lax.dot_general(
                q_rows[rows_b, hs], k_rows[keys, hs], (((1,), (1,)), ((), ())),
                preferred_element_type=jnp.float32,
            )
            key_pos = lax.broadcasted_iota(jnp.int32, (1, count), 1)
            scores = scores + jnp.where(key_pos < length, 0.0, -1e30)
            edge = jnp.where(below, scores[:, b * step_rows :], -1e30)
            scores = edge if b == 0 else jnp.concatenate([scores[:, : b * step_rows], edge], 1)
            terms = jnp.exp2((scores - jnp.max(scores, axis=-1, keepdims=True)) * exponent)
            mixed = jnp.dot(
                terms.astype(jnp.bfloat16), v_rows[keys, hs], preferred_element_type=jnp.float32
            ) / jnp.sum(terms, axis=-1, keepdims=True)
            row = lax.broadcasted_iota(jnp.int32, (step_rows, HD), 0) + b * step_rows
            attended[rows_b, hs] = jnp.where(row < length, mixed, 0.0).astype(jnp.bfloat16)
        return carry

    lax.fori_loop(0, token_rows // seq_len * heads, attend, 0, unroll=2)

    def drain(step, carry):
        for u in range(STREAMS):
            ring(u, step).wait_send()
        return carry

    lax.fori_loop(1, chips, drain, 0)

    def drain_sib(step, carry):
        for u in range(STREAMS):
            sib(u, step, core).wait_send()
        return carry

    lax.fori_loop(0, chips, drain_sib, 0)
    for kind in (1, 0):
        for slot in range(CAP):
            for direction in range(2):
                send_page(kind, direction, slot).wait()
            keep_page(kind, slot).wait()


def body(tokens, qkv_master, q_gain, k_gain, lengths, page_holder, page_slot):
    req_dev, seq_len, model_width = tokens.shape
    row_share, _, q_local = qkv_master.shape
    half = q_local // 2
    count = lax.axis_size("req")
    chips = count // 2
    rows = req_dev * seq_len
    token_rows = tokens.reshape(rows, model_width)

    frequency = np.float32(rope_theta) ** (-np.arange(HD // 2, dtype=np.float32) * np.float32(2.0 / HD))
    angles = np.arange(seq_len, dtype=np.float32)[:, None] * frequency[None, :]
    cosine, sine = np.cos(angles), np.sin(angles)
    cosine = jnp.asarray(np.concatenate([cosine, cosine], -1), jnp.float32)
    sine = jnp.asarray(np.concatenate([-sine, sine], -1), jnp.float32)

    page_count = seq_len // PAGE
    home = lax.axis_index("req")
    live = (jnp.arange(page_count) * PAGE)[None, :] < lengths[:, None]
    offset = (page_holder - home + 1 + count) % count - 1
    target = jnp.where(live, (offset + 1) * CAP + page_slot, -1).reshape(-1)
    match = target[None, :] == jnp.arange(SLOTS)[:, None]
    chosen = match.astype(jnp.float32).reshape(-1)

    vmem = pl.BlockSpec(memory_space=pltpu.VMEM)
    smem = pl.BlockSpec(memory_space=pltpu.SMEM)
    dma = pltpu.SemaphoreType.DMA
    attended, cache = pl.pallas_call(
        functools.partial(prefill_kernel, count, q_local * lax.axis_size("tp"), seq_len),
        out_shape=(
            jax.ShapeDtypeStruct((rows, q_local), jnp.bfloat16),
            jax.ShapeDtypeStruct((SLOTS, 2, PAGE, q_local), jnp.bfloat16),
        ),
        in_specs=[smem] * 2 + [vmem] * 6,
        out_specs=(vmem, pl.BlockSpec(memory_space=pl.ANY)),
        scratch_shapes=[
            pltpu.VMEM((STREAMS, model_width, half), jnp.bfloat16),
            pltpu.VMEM((STREAMS, rows, half), jnp.float32),
            pltpu.VMEM((rows, q_local), jnp.bfloat16),
            pltpu.VMEM((rows, q_local), jnp.bfloat16),
            pltpu.VMEM((rows, q_local), jnp.bfloat16),
            pltpu.VMEM((2, 3, CAP, PAGE, q_local), jnp.bfloat16),
            pltpu.VMEM((8, rows), jnp.float32),
            pltpu.VMEM((8, rows), jnp.float32),
            dma((STREAMS, chips)), dma((STREAMS, chips)),
            dma((STREAMS, chips)), dma((STREAMS, chips)),
            dma, dma,
            dma((2, 2, CAP)), dma((2, 2, CAP)), dma((2, CAP)),
        ],
        compiler_params=pltpu.CompilerParams(
            collective_id=0, has_side_effects=True, vmem_limit_bytes=VMEM_LIMIT
        ),
    )(lengths, chosen, token_rows, qkv_master.transpose(1, 0, 2), cosine, sine, q_gain[None, :], k_gain[None, :])
    return attended.reshape(req_dev, seq_len, q_local), cache


def solution(mesh):
    in_specs = (
        P("req", None, None),
        P("req", None, "tp"),
        P("tp"),
        P("tp"),
        P("req"),
        P("req", None),
        P("req", None),
    )
    out_specs = (P("req", None, "tp"), P("req", None, None, "tp"))
    return jax.shard_map(body, mesh=mesh, in_specs=in_specs, out_specs=out_specs, check_vma=False)
```
